256 devices in a mesh: row: 8 (over x, core), col: 32 (over z, y).
Axes of the slice: x: 4, y: 4, z: 8, core: 2. Of those that a mesh axis runs over, the one named last changes fastest.
Arguments:
- hidden_states: bfloat16 [1024, 8192], P('col', 'row'), may hold values from -60 to 60
- head_weight: bfloat16 [8192, 65536], P('row', 'col'), may hold values from -1 to 1
- teacher_logits: bfloat16 [1024, 65536], P('row', 'col'), may hold values from -60 to 400
Outputs:
- loss: float32 [], replicated
- head_grad: bfloat16 [8192, 65536], P('row', 'col')
- hidden_grad: bfloat16 [1024, 8192], P('col', 'row')
The draws below stay inside these ranges and needn't reach their ends.
All inputs are finite; a program needn't handle non-finite values.
Results may differ from the reference program's by a relative error of at most 0.025.
Values may be sent and summed in bfloat16 or wider, within the bound.
No kernel may reach another device: no remote copies, remote signals or barrier semaphores. Data moves between devices by JAX's collectives and lax.ppermute only.
A program may use at most 64 MiB of HBM per device.

```python
import jax
import jax.numpy as jnp

D = 8192
VOCAB = 65536
TOKENS = 1024


def column_scales(key):
    base = jax.random.fold_in(key, 101)
    return jnp.exp(jax.random.uniform(jax.random.fold_in(base, 1), (1, VOCAB), jnp.float32, jnp.log(0.5), jnp.log(5.0)))


def head_values(key):
    base = jax.random.fold_in(key, 101)
    col_scale = column_scales(key)
    normal_part = jnp.clip(jax.random.normal(jax.random.fold_in(base, 2), (D, VOCAB), jnp.float32), -5.0, 5.0)
    noise = normal_part
    return jnp.clip(noise * col_scale * (3.0 / jnp.sqrt(jnp.float32(D))), -1.0, 1.0)


def top_columns(key):
    return jax.random.randint(jax.random.fold_in(key, 211), (TOKENS,), 0, VOCAB)


def top_margins(key):
    offsets = jax.random.uniform(jax.random.fold_in(key, 223), (TOKENS,), jnp.float32, 0.2, 1.2)
    return jnp.log(jnp.float32(VOCAB)) + offsets


def draw_head_weight(key, part):
    return head_values(key).astype(jnp.bfloat16)


def draw_hidden_states(key, part):
    heads = head_values(key)
    scales = column_scales(key)[0]
    chosen_columns = top_columns(key)
    margins = top_margins(key)
    chosen = heads[:, chosen_columns].T
    pick_scale = scales[chosen_columns][:, None]
    aligned_top = margins[:, None] * chosen / (9.0 * pick_scale * pick_scale)
    key = jax.random.fold_in(key, 7)
    noise_scale = 0.03 * jnp.exp(jax.random.uniform(jax.random.fold_in(key, 1), (TOKENS, 1), jnp.float32, jnp.log(1.0 / 3.0), 0.0))
    normal_part = jnp.clip(jax.random.normal(jax.random.fold_in(key, 2), (TOKENS, D), jnp.float32), -5.0, 5.0)
    states = normal_part * noise_scale + aligned_top
    return states.astype(jnp.bfloat16)


def draw_teacher_logits(key, part):
    chosen_columns = top_columns(key)
    margins = top_margins(key)
    key = jax.random.fold_in(key, 13)
    row_scale = jnp.exp(jax.random.uniform(jax.random.fold_in(key, 1), (TOKENS, 1), jnp.float32, jnp.log(0.3), jnp.log(3.0)))
    noise = jnp.clip(jax.random.normal(jax.random.fold_in(key, 2), (TOKENS, VOCAB), jnp.float32), -5.0, 5.0)
    logits = 3.0 * row_scale * noise
    logits = logits.at[jnp.arange(TOKENS), chosen_columns].set(margins)
    return logits.astype(jnp.bfloat16)


def setup_inputs(seed: int = 0) -> dict:
    splits = jax.random.split(jax.random.key(seed), 4)
    return {
        "hidden_states": draw_hidden_states(jax.random.fold_in(splits[3], 71), 0),
        "head_weight": draw_head_weight(jax.random.fold_in(splits[3], 71), 0),
        "teacher_logits": draw_teacher_logits(jax.random.fold_in(splits[3], 71), 0),
    }


def reference(hidden_states, head_weight, teacher_logits):
    student = jnp.dot(hidden_states, head_weight, preferred_element_type=jnp.float32)
    teacher = teacher_logits.astype(jnp.float32)
    top_s = jnp.max(student, axis=1, keepdims=True)
    top_t = jnp.max(teacher, axis=1, keepdims=True)
    shifted = jnp.exp(student - top_s)
    total_s = jnp.sum(shifted, axis=1, keepdims=True)
    spread = jnp.sum(shifted * (student - teacher), axis=1, keepdims=True)
    total_t = jnp.sum(jnp.exp(teacher - top_t), axis=1, keepdims=True)
    lse_s = top_s + jnp.log(total_s)
    lse_t = top_t + jnp.log(total_t)
    kl_rows = spread / total_s - lse_s + lse_t
    loss = jnp.sum(kl_rows) / TOKENS
    grad = (16.0 * jnp.exp(student - lse_s) * (student - teacher - lse_s + lse_t - kl_rows)).astype(jnp.bfloat16)
    head_grad = jnp.dot(hidden_states.T, grad, preferred_element_type=jnp.float32).astype(jnp.bfloat16)
    hidden_grad = jnp.dot(grad, head_weight.T, preferred_element_type=jnp.float32).astype(jnp.bfloat16)
    return loss, head_grad, hidden_grad
```

```python
import jax
import jax.numpy as jnp
from jax import lax
from jax.sharding import Mesh, PartitionSpec as P

NX, NC, NZ, NY = 4, 2, 8, 4
F32, BF16 = jnp.float32, jnp.bfloat16
GROUPS = ((0,), (-1, 1), (-2, 2), (-3, 3), (4,))
ORDER = tuple(d for g in GROUPS for d in g)
TAILS = ((4, -3, 3, -2), (2, -1, 1, 0))


def from_offset(value, axis, offset, size):
    return lax.ppermute(value, axis, [((i + offset) % size, i) for i in range(size)])


def swap(value):
    return lax.ppermute(value, "c", [(0, 1), (1, 0)])


def turn(value, start, axis=0):
    size = value.shape[axis]
    return lax.dynamic_slice_in_dim(jnp.concatenate([value, value], axis), start, size, axis)


def merge(parts):
    top_s = jnp.max(parts[:, 0], axis=0)
    top_t = jnp.max(parts[:, 3], axis=0)
    scale_s = jnp.exp(parts[:, 0] - top_s)
    scale_t = jnp.exp(parts[:, 3] - top_t)
    total_s = jnp.sum(parts[:, 1] * scale_s, axis=0)
    spread = jnp.sum(parts[:, 2] * scale_s, axis=0)
    total_t = jnp.sum(parts[:, 4] * scale_t, axis=0)
    zero = jnp.zeros_like(top_s)
    return jnp.stack([top_s, total_s, spread, top_t, total_t, zero, zero, zero])


def per_device(h, w, t):
    x, c, z, y = (lax.axis_index(a) for a in ("x", "c", "z", "y"))
    tokens, width = h.shape
    half = w.shape[1] // 2

    near = jnp.stack([h] + [from_offset(h, "y", s, NY) for s in (1, 2, 3)])
    near = turn(near, (x - y) % NY)

    w_mine = lax.dynamic_slice_in_dim(w, c * half, half, 1)
    w_theirs = lax.dynamic_slice_in_dim(w, (1 - c) * half, half, 1)
    w_deep = swap(w_theirs)
    t_mine = lax.dynamic_slice_in_dim(t, c * half, half, 1)
    t_deep = swap(lax.dynamic_slice_in_dim(t, (1 - c) * half, half, 1))

    pair = jnp.where(c == 0, jnp.stack([t_mine, t_deep]), jnp.stack([t_deep, t_mine]))
    pair = turn(pair.reshape(2, NY, tokens, half), x, 1)
    teach = [pair[:, 0]] + [from_offset(pair[:, NX - s], "x", s, NX) for s in (1, 2, 3)]
    teach = jnp.concatenate(teach, 0)
    teach = turn(teach, (z - 2 * x) % NZ)

    blocks = {0: near}
    up = down = near
    for s in (1, 2, 3):
        up, down = from_offset(up, "z", -1, NZ), from_offset(down, "z", 1, NZ)
        blocks[-s], blocks[s] = up, down
    blocks[4] = jnp.concatenate(
        [from_offset(up[:2], "z", -1, NZ), from_offset(down[2:], "z", 1, NZ)], 0
    )

    students, stats = {}, {}
    for group in GROUPS:
        n = len(group)
        mine = jnp.stack([blocks[d] for d in group])
        deep = swap(mine)
        flat = (n * NY * tokens, width)
        part = jnp.dot(mine.reshape(flat), w_mine, preferred_element_type=F32) + jnp.dot(
            deep.reshape(flat), w_deep, preferred_element_type=F32
        )
        part = part.reshape(n, NX, tokens, half)
        lo, hi = part[:, 2, : tokens // 2], part[:, 2, tokens // 2 :]
        from_left = from_offset(lo, "x", -1, NX)
        from_right = from_offset(hi, "x", 1, NX)
        to_right = jnp.concatenate(
            [part[:, 1, : tokens // 2] + from_left, part[:, 1, tokens // 2 :]], 1
        )
        to_left = jnp.concatenate(
            [part[:, 3, : tokens // 2], part[:, 3, tokens // 2 :] + from_right], 1
        )
        student = (
            part[:, 0] + from_offset(to_right, "x", -1, NX) + from_offset(to_left, "x", 1, NX)
        )
        teacher = jnp.stack([teach[d % NZ] for d in group]).astype(F32)
        top_s = jnp.max(student, axis=2, keepdims=True)
        top_t = jnp.max(teacher, axis=2, keepdims=True)
        shifted = jnp.exp(student - top_s)
        rows = (
            top_s[..., 0],
            jnp.sum(shifted, axis=2),
            jnp.sum(shifted * (student - teacher), axis=2),
            top_t[..., 0],
            jnp.sum(jnp.exp(teacher - top_t), axis=2),
        )
        for i, d in enumerate(group):
            students[d] = student[i]
            stats[d] = [r[i] for r in rows]

    mine = jnp.stack([jnp.stack([stats[d if d < 5 else d - NZ][r] for d in range(NZ)]) for r in range(5)])
    mine = jnp.pad(turn(mine, (-z) % NZ, 1), ((0, 3), (0, 0), (0, 0))).reshape(8, NZ * tokens)
    cores = [mine, swap(mine)]
    both = jnp.where(c == 0, jnp.stack(cores), jnp.stack(cores[::-1]))
    mine = merge(both)
    mine = merge(turn(jnp.stack([mine] + [from_offset(mine, "y", s, NY) for s in range(1, NY)]), (-y) % NY))
    mine = merge(turn(jnp.stack([mine] + [from_offset(mine, "z", s, NZ) for s in range(1, NZ)]), (-z) % NZ))
    lse_s = mine[0] + jnp.log(mine[1])
    lse_t = mine[3] + jnp.log(mine[4])
    kl = mine[2] / mine[1] - lse_s + lse_t
    kl_sum = jnp.full((8, 128), jnp.sum(kl))
    kl_sum = turn(jnp.stack([kl_sum] + [from_offset(kl_sum, "x", s, NX) for s in range(1, NX)]), (-x) % NX)
    loss = jnp.sum(kl_sum[:, 0, 0]) / (NX * NZ * tokens)
    lse_row = turn(lse_s.reshape(NZ, tokens), z)
    add_row = turn((lse_t - lse_s - kl).reshape(NZ, tokens), z)

    grads = {}
    for d in ORDER:
        student, teacher = students[d], teach[d % NZ].astype(F32)
        lse, add = lse_row[d % NZ][:, None], add_row[d % NZ][:, None]
        grads[d] = (16.0 * jnp.exp(student - lse) * (student - teacher + add)).astype(BF16)

    panel, grads_mine, grads_deep, sums = [], [], [], []
    for tail in TAILS:
        n = len(tail)
        own = jnp.stack([grads[d] for d in tail])
        mine = jnp.stack([own] + [from_offset(own, "x", s, NX) for s in (1, 2, 3)], 1)
        deep = swap(mine)
        flat = (n * NY * tokens, half)
        mine, deep = mine.reshape(flat), deep.reshape(flat)
        grads_mine.append(mine)
        grads_deep.append(deep)
        panel += [blocks[d].reshape(NY * tokens, width) for d in tail]
        out = lax.dot_general(
            mine, w_mine, (((1,), (1,)), ((), ())), preferred_element_type=F32
        ) + lax.dot_general(deep, w_theirs, (((1,), (1,)), ((), ())), preferred_element_type=F32)
        out = out.reshape(n, NX, tokens, width)
        total = lax.dynamic_index_in_dim(out, (y - x) % NY, 1, False)
        for s in (1, 2, 3):
            block = lax.dynamic_index_in_dim(out, (y + s - x) % NY, 1, False).astype(BF16)
            total = total + from_offset(block, "y", -s, NY).astype(F32)
        for i, d in enumerate(tail):
            sums.append(total[i] if d == 0 else from_offset(total[i].astype(BF16), "z", -d, NZ).astype(F32))
    hidden_grad = sums[0]
    for s in sums[1:]:
        hidden_grad = hidden_grad + s

    panel = jnp.concatenate(panel, 0)
    mine, deep = jnp.concatenate(grads_mine, 0), jnp.concatenate(grads_deep, 0)
    both = jnp.where(c == 0, jnp.concatenate([mine, deep], 1), jnp.concatenate([deep, mine], 1))
    head_grad = jnp.dot(panel.T, both, preferred_element_type=F32)
    return loss, head_grad.astype(BF16), hidden_grad.astype(BF16)


def solution(mesh):
    fine = Mesh(mesh.devices.reshape(NX, NC, NZ, NY), ("x", "c", "z", "y"))
    row, col = ("x", "c"), ("z", "y")
    return jax.shard_map(
        per_device,
        mesh=fine,
        in_specs=(P(col, row), P(row, col), P(row, col)),
        out_specs=(P(), P(row, col), P(col, row)),
        check_vma=False,
    )
```

```python
import jax
import jax.numpy as jnp
from jax import lax
from jax.experimental import pallas as pl
from jax.experimental.pallas import tpu as pltpu
from jax.sharding import Mesh, PartitionSpec as P

NX, NC, NZ, NY = 4, 2, 8, 4
F32, BF16 = jnp.float32, jnp.bfloat16
MIB = 2**20
ORDER = (0, -1, 1, -2, 2, -3, 3, 4)


def from_offset(value, axis, offset, size):
    return lax.ppermute(value, axis, [((i + offset) % size, i) for i in range(size)])


def swap(value):
    return lax.ppermute(value, "c", [(0, 1), (1, 0)])


def ordered(*values):
    return lax.optimization_barrier(values)


def held(*trees):
    leaves, shape = jax.tree.flatten(trees)
    return jax.tree.unflatten(shape, ordered(*leaves))


def call(kernel, out_shape, place, *args, scratch=(), aliases=None, vmem=10 * MIB):
    in_vmem = pl.BlockSpec(memory_space=pltpu.VMEM)
    return pl.pallas_call(
        kernel,
        out_shape=out_shape,
        in_specs=[pl.BlockSpec(memory_space=pltpu.SMEM)] + [in_vmem] * len(args),
        out_specs=jax.tree.map(lambda _: in_vmem, out_shape),
        scratch_shapes=list(scratch),
        input_output_aliases=aliases or {},
        compiler_params=pltpu.CompilerParams(vmem_limit_bytes=vmem),
        cost_estimate=pl.CostEstimate(flops=0, bytes_accessed=0, transcendentals=0),
    )(place, *args)


def by_owner(place, values):
    def kernel(place, *refs):
        for s, value in enumerate(refs[:-1]):
            refs[-1][lax.rem(s + NX - place[2], NX)] = value[...]

    shape = (len(values), *values[0].shape)
    return call(kernel, jax.ShapeDtypeStruct(shape, values[0].dtype), place, *values)


def student_parts(place, base, mine, deep, w_mine, w_deep, before):
    n, (owners, tokens, width) = len(mine), mine[0].shape
    half = w_deep.shape[1]
    tile = half // 4
    rows = len(ORDER) * tokens
    before = before or []

    def kernel(place, *refs):
        mine, deep = refs[:n], refs[n : 2 * n]
        w_mine, w_deep = refs[2 * n : 2 * n + 2]
        own, *outs = refs[2 * n + 2 + len(before) :]

        def stacked(blocks):
            return jnp.concatenate([b[...].reshape(owners * tokens, width) for b in blocks], 0)

        lhs, lhs_deep = stacked(mine), stacked(deep)
        for g in range(4):
            cols = slice(g * tile, (g + 1) * tile)
            part = jnp.dot(lhs, w_mine[:, cols], preferred_element_type=F32)
            part += jnp.dot(lhs_deep, w_deep[:, cols], preferred_element_type=F32)
            for j in range(owners):
                out = own if j == 0 else outs[2 * (j - 1) + g // 2]
                col = g * tile if j == 0 else g % 2 * tile
                for i in range(n):
                    row = (i * owners + j) * tokens
                    out[(base + i) * tokens : (base + i + 1) * tokens, col : col + tile] = part[
                        row : row + tokens
                    ]

    return call(
        kernel,
        [jax.ShapeDtypeStruct((rows, half), F32)]
        + [jax.ShapeDtypeStruct((rows, half // 2), F32)] * (2 * owners - 2),
        place,
        *mine,
        *deep,
        w_mine,
        w_deep,
        *before,
        aliases={3 + 2 * n + k: k for k in range(len(before))},
    )


def half_of(place, value, mine):
    half = value.shape[-1] // 2

    def kernel(place, value, out):
        core = place[0] if mine else 1 - place[0]
        out[...] = value[..., pl.ds(pl.multiple_of(core * half, half), half)]

    return call(kernel, jax.ShapeDtypeStruct((*value.shape[:-1], half), value.dtype), place, value)


def columns_of(place, value, other):
    rows, half = value.shape[0], value.shape[1] // 2

    def kernel(place, value, out, sem):
        core = 1 - place[0] if other else place[0]
        columns = value.at[:, pl.ds(pl.multiple_of(core * half, half), half)]
        copy = pltpu.make_async_copy(columns, out, sem)
        copy.start()
        copy.wait()

    return pl.pallas_call(
        kernel,
        out_shape=jax.ShapeDtypeStruct((rows, half), value.dtype),
        in_specs=[pl.BlockSpec(memory_space=pltpu.SMEM), pl.BlockSpec(memory_space=pl.ANY)],
        out_specs=pl.BlockSpec(memory_space=pltpu.VMEM),
        scratch_shapes=[pltpu.SemaphoreType.DMA],
        cost_estimate=pl.CostEstimate(flops=0, bytes_accessed=0, transcendentals=0),
    )(place, value)


def teacher_block(place, distance, mine, theirs):
    z = lax.rem(place[1] + distance, NZ)
    back = lax.rem(place[3] + NX - lax.div(z, 2), NX)
    return jnp.where(lax.rem(z, 2) == place[0], mine[back], theirs[back]).astype(F32)


def row_statistics(place, own, terms, teachers):
    rows, half = own.shape
    tokens = rows // len(ORDER)

    def kernel(place, own, a, b, c, d, teacher, theirs, student, out, held):
        lane = lax.broadcasted_iota(jnp.int32, (tokens, 128), 1)
        for i, distance in enumerate(ORDER):
            at = slice(i * tokens, (i + 1) * tokens)
            s = own[at, :] + jnp.concatenate([a[at, :] + b[at, :], c[at, :] + d[at, :]], 1)
            t = teacher_block(place, distance % NZ, teacher, theirs)
            top_s = jnp.max(s, axis=1, keepdims=True)
            top_t = jnp.max(t, axis=1, keepdims=True)
            e = jnp.exp(s - top_s)
            values = (
                top_s,
                jnp.sum(e, axis=1, keepdims=True),
                jnp.sum(e * (s - t), axis=1, keepdims=True),
                top_t,
                jnp.sum(jnp.exp(t - top_t), axis=1, keepdims=True),
            )
            stats = jnp.zeros((tokens, 128), F32)
            for k, v in enumerate(values):
                stats = jnp.where(lane == k, v, stats)
            student[at, :] = s
            z = lax.rem(place[1] + distance % NZ, NZ)
            held[pl.ds(pl.multiple_of(z * tokens, tokens), tokens), :] = stats
        out[...] = held[...].T[:8]

    return call(
        kernel,
        [jax.ShapeDtypeStruct((rows, half), F32), jax.ShapeDtypeStruct((8, rows), F32)],
        place,
        own,
        *terms,
        *teachers,
        scratch=[pltpu.VMEM((rows, 128), F32)],
    )


def merged(parts):
    top_s = jnp.max(parts[0], axis=0, keepdims=True)
    top_t = jnp.max(parts[3], axis=0, keepdims=True)
    scale_s, scale_t = jnp.exp(parts[0] - top_s), jnp.exp(parts[3] - top_t)
    return (
        top_s,
        jnp.sum(parts[1] * scale_s, axis=0, keepdims=True),
        jnp.sum(parts[2] * scale_s, axis=0, keepdims=True),
        top_t,
        jnp.sum(parts[4] * scale_t, axis=0, keepdims=True),
    )


def merge_cores(place, mine, theirs, copies):
    def kernel(place, mine, theirs, out):
        first = place[0] == 0
        a = jnp.where(first, mine[...], theirs[...])
        b = jnp.where(first, theirs[...], mine[...])
        rows = merged([jnp.concatenate([a[k : k + 1], b[k : k + 1]], 0) for k in range(5)])
        row = lax.broadcasted_iota(jnp.int32, a.shape, 0)
        value = jnp.zeros(a.shape, F32)
        for k, v in enumerate(rows):
            value = jnp.where(row == k, v, value)
        for k in range(copies):
            out[k] = value

    return call(kernel, jax.ShapeDtypeStruct((copies, *mine.shape), F32), place, mine, theirs)


def gradients(place, shares, student, teachers):
    rows, half = student.shape
    tokens = rows // NZ

    def kernel(place, shares, student, teacher, theirs, out, kl_sum, held):
        top_s, total_s, spread, top_t, total_t = merged([shares[:, k, :] for k in range(5)])
        lse_s, lse_t = top_s + jnp.log(total_s), top_t + jnp.log(total_t)
        kl = spread / total_s - lse_s + lse_t
        kl_sum[...] = jnp.broadcast_to(jnp.sum(kl, axis=1, keepdims=True), kl_sum.shape)
        row = lax.broadcasted_iota(jnp.int32, (128, rows), 0)
        held[...] = jnp.where(row == 0, lse_s, jnp.where(row == 1, lse_t - lse_s - kl, 0.0)).T
        for i, d in enumerate(ORDER):
            z = lax.rem(place[1] + d % NZ, NZ)
            per_row = held[pl.ds(pl.multiple_of(z * tokens, tokens), tokens), :]
            lse, add = per_row[:, 0:1], per_row[:, 1:2]
            at = slice(i * tokens, (i + 1) * tokens)
            s = student[at, :]
            t = teacher_block(place, d % NZ, teacher, theirs)
            out[at, :] = (16.0 * jnp.exp(s - lse) * (s - t + add)).astype(out.dtype)

    return call(
        kernel,
        [jax.ShapeDtypeStruct((rows, half), BF16), jax.ShapeDtypeStruct((8, 128), F32)],
        place,
        shares,
        student,
        *teachers,
        scratch=[pltpu.VMEM((rows, 128), F32)],
    )


def panel_transposed(place, blocks):
    owners, tokens, width = blocks[0].shape
    total = len(blocks) * owners * tokens

    def kernel(place, *refs):
        held, out = refs[:-1], refs[-1]
        for j in range(owners):
            rows = jnp.concatenate([b[j] for b in held], 0)
            out[:, j * rows.shape[0] : (j + 1) * rows.shape[0]] = rows.T

    return call(kernel, jax.ShapeDtypeStruct((width, total), BF16), place, *blocks)


def hidden_parts(place, mine, deep, w_mine, w_theirs, tile=256):
    rows, half = mine[0].shape
    width = w_mine.shape[0]
    tile = min(tile, width // 2)
    kept = ((0, 0), (0, 1), (1, 0), (3, 1))

    def kernel(place, *refs):
        mine, deep = refs[:NX], refs[NX : 2 * NX]
        w_mine, w_theirs, *outs = refs[2 * NX : 2 * NX + 2 + 2 * NY]
        by_y, by_y_deep = refs[2 * NX + 2 + 2 * NY :]
        for j in range(NX):
            s = lax.rem(place[2] + j, NY)
            by_y[s] = mine[j][...]
            by_y_deep[s] = deep[j][...]
        contract = (((1,), (1,)), ((), ()))
        flat = (NX * rows, half)
        lhs, lhs_deep = by_y[...].reshape(flat), by_y_deep[...].reshape(flat)
        for g in range(width // tile):
            at = slice(g * tile, (g + 1) * tile)
            out = lax.dot_general(lhs, w_mine[at, :], contract, preferred_element_type=F32)
            out += lax.dot_general(lhs_deep, w_theirs[at, :], contract, preferred_element_type=F32)
            k, col = divmod(g * tile, width // 2)
            for s in range(NY):
                ref = outs[2 * s + k]
                ref[:, col : col + tile] = out[s * rows : (s + 1) * rows].astype(ref.dtype)

    return call(
        kernel,
        [
            jax.ShapeDtypeStruct((rows, width // 2), F32 if (s, k) in kept else BF16)
            for s in range(NY)
            for k in range(2)
        ],
        place,
        *mine,
        *deep,
        w_mine,
        w_theirs,
        scratch=[pltpu.VMEM((NX, rows, half), BF16)] * 2,
    )


def head_product(place, panel, grads, other, before=None, tile=256):
    width, total = panel.shape
    n, (rows, half) = len(grads), grads[0].shape
    tile = min(tile, width)
    before = [] if before is None else [before]

    def kernel(place, panel, *refs):
        grads, out, held = refs[:n], refs[n + len(before)], refs[-1]

        @pl.when(pl.program_id(0) == 0)
        def _():
            for k in range(n):
                held[k * rows : (k + 1) * rows, :] = grads[k][...]

        out[...] = jnp.dot(panel[...], held[...], preferred_element_type=F32).astype(out.dtype)

    in_vmem = pl.BlockSpec(memory_space=pltpu.VMEM)
    return pl.pallas_call(
        kernel,
        out_shape=jax.ShapeDtypeStruct((width, 2 * half), BF16),
        grid_spec=pltpu.PrefetchScalarGridSpec(
            num_scalar_prefetch=1,
            grid=(width // tile,),
            in_specs=[pl.BlockSpec((tile, total), lambda i, place: (i, 0))]
            + [in_vmem] * n
            + [pl.BlockSpec(memory_space=pl.ANY)] * len(before),
            out_specs=pl.BlockSpec(
                (tile, half), lambda i, place: (i, other + place[0] - 2 * other * place[0])
            ),
            scratch_shapes=[pltpu.VMEM((total, half), BF16)],
        ),
        input_output_aliases={2 + n: 0} if before else {},
        compiler_params=pltpu.CompilerParams(vmem_limit_bytes=24 * MIB),
        cost_estimate=pl.CostEstimate(flops=0, bytes_accessed=0, transcendentals=0),
    )(place, panel, *grads, *before)


def per_device(h, w, t):
    x, c, z, y = (lax.axis_index(a) for a in ("x", "c", "z", "y"))
    tokens, width = h.shape
    half = w.shape[1] // 2
    place = jnp.stack([c, z, (x - y) % NY, x]).astype(jnp.int32)

    near = [h] + [from_offset(h, "y", s, NY) for s in (1, 2, 3)]
    teacher = [lax.dynamic_slice_in_dim(t, lax.rem(x + s, NX) * tokens, tokens, 0) for s in range(NX)]
    teacher = [teacher[0]] + [from_offset(teacher[s], "x", -s, NX) for s in (1, 2, 3)]
    w_theirs = columns_of(place, w, True)
    near, w_theirs = held(near, w_theirs)
    w_deep = swap(w_theirs)
    near = by_owner(place, near)
    w, near = ordered(w, near)
    w_mine = columns_of(place, w, False)

    def products(new, parts):
        base = len(blocks)
        blocks.extend(new)
        return student_parts(place, base, new, [swap(b) for b in new], w_mine, w_deep, parts)

    blocks, parts = [], None
    up, down = from_offset(near, "z", -1, NZ), from_offset(near, "z", 1, NZ)
    up, down, w_deep, w_mine = held(up, down, w_deep, w_mine)
    new = [near, up, down]
    for step in (2, 3):
        up, down = from_offset(up, "z", -1, NZ), from_offset(down, "z", 1, NZ)
        parts = products(new, parts)
        if step == 2:
            up, down, parts, teacher = held(up, down, parts, teacher)
        else:
            up, down, parts = held(up, down, parts)
        new = [up, down]
    far = [from_offset(up[:2], "z", -1, NZ), from_offset(down[2:], "z", 1, NZ)]
    teacher = jnp.stack(teacher)
    teachers = half_of(place, teacher, True), swap(half_of(place, teacher, False))
    far, teachers = held(far, teachers)
    parts = products(new + [jnp.concatenate(far, 0)], parts)

    own, right_a, right_b, two_a, two_b, left_a, left_b = parts
    two_a, two_b = from_offset(two_a, "x", -1, NX), from_offset(two_b, "x", 1, NX)
    two_a, two_b, panel = ordered(two_a, two_b, panel_transposed(place, blocks))
    terms = (
        from_offset(right_a + two_a, "x", -1, NX),
        from_offset(left_a, "x", 1, NX),
        from_offset(right_b, "x", -1, NX),
        from_offset(left_b + two_b, "x", 1, NX),
    )
    student, mine = row_statistics(place, own, terms, teachers)

    copies = merge_cores(place, mine, swap(mine), NZ * NY)
    shares = lax.all_to_all(copies, ("z", "y"), 0, 0, tiled=True)
    grad, kl_sum = gradients(place, shares, student, teachers)

    mine = [grad] + [from_offset(grad, "x", s, NX) for s in (1, 2, 3)]
    kl_sum = kl_sum + lax.ppermute(kl_sum, "x", [(i ^ 1, i) for i in range(NX)])
    kl_sum, mine[2] = ordered(kl_sum, mine[2])
    deep = [swap(g) for g in mine]
    sums = hidden_parts(place, mine, deep, w_mine, w_theirs)
    own, one, two, three = list(sums[:2]), sums[2:4], sums[4:6], sums[6:]
    two = [from_offset(two[0], "y", -1, NY), from_offset(two[1], "y", 1, NY)]
    head_grad = head_product(place, panel, mine, 0)
    came = [[None, from_offset(one[1], "y", -1, NY)], [from_offset(three[0], "y", 1, NY), None]]
    one = (one[0] + two[0].astype(F32)).astype(BF16)
    three = (three[1] + two[1].astype(F32)).astype(BF16)
    came[0][0], came[1][1] = from_offset(one, "y", -1, NY), from_offset(three, "y", 1, NY)
    head_grad = head_product(place, panel, deep, 1, head_grad)
    came, head_grad, kl_sum = held(came, head_grad, kl_sum)
    kl_sum = kl_sum + lax.ppermute(kl_sum, "x", [(i ^ 2, i) for i in range(NX)])
    loss = kl_sum[0, 0] / (NX * NZ * tokens)
    total = jnp.concatenate(
        [own[k] + came[0][k].astype(F32) + came[1][k].astype(F32) for k in range(2)], 1
    )
    hidden_grad = None
    for i, d in enumerate(ORDER):
        piece = total[i * tokens : (i + 1) * tokens]
        if d:
            piece = from_offset(piece.astype(BF16), "z", -d, NZ).astype(F32)
        hidden_grad = piece if hidden_grad is None else hidden_grad + piece
    return loss, head_grad, hidden_grad.astype(BF16)


def solution(mesh):
    fine = Mesh(mesh.devices.reshape(NX, NC, NZ, NY), ("x", "c", "z", "y"))
    row, col = ("x", "c"), ("z", "y")
    return jax.shard_map(
        per_device,
        mesh=fine,
        in_specs=(P(col, row), P(row, col), P(row, col)),
        out_specs=(P(), P(row, col), P(col, row)),
        check_vma=False,
    )
```

```python
import jax
import jax.numpy as jnp
from jax import lax
from jax.experimental import pallas as pl
from jax.experimental.pallas import tpu as pltpu
from jax.sharding import Mesh, PartitionSpec as P

NX, NC, NZ, NY = 4, 2, 8, 4
F32, BF16 = jnp.float32, jnp.bfloat16
MIB = 2**20


def from_offset(value, axis, offset, size):
    return lax.ppermute(value, axis, [((i + offset) % size, i) for i in range(size)])


def swap(value):
    return lax.ppermute(value, "c", [(0, 1), (1, 0)])


def ordered(*values):
    return lax.optimization_barrier(values)


def held(*trees):
    leaves, shape = jax.tree.flatten(trees)
    return jax.tree.unflatten(shape, ordered(*leaves))


def call(kernel, out_shape, place, *args, scratch=(), aliases=None, vmem=10 * MIB):
    in_vmem = pl.BlockSpec(memory_space=pltpu.VMEM)
    return pl.pallas_call(
        kernel,
        out_shape=out_shape,
        in_specs=[pl.BlockSpec(memory_space=pltpu.SMEM)] + [in_vmem] * len(args),
        out_specs=jax.tree.map(lambda _: in_vmem, out_shape),
        scratch_shapes=list(scratch),
        input_output_aliases=aliases or {},
        compiler_params=pltpu.CompilerParams(vmem_limit_bytes=vmem),
        cost_estimate=pl.CostEstimate(flops=0, bytes_accessed=0, transcendentals=0),
    )(place, *args)


def by_y(place, values):
    def kernel(place, *refs):
        for s, value in enumerate(refs[:-1]):
            refs[-1][lax.rem(s + place[2], NY)] = value[...]

    shape = (len(values), *values[0].shape)
    return call(kernel, jax.ShapeDtypeStruct(shape, values[0].dtype), place, *values)


def student_parts(place, distances, mine, deep, w_mine, w_deep, before, last):
    n, (_, tokens, width) = len(mine), mine[0].shape
    half = w_deep.shape[1]
    tile = half // 4
    rows = NY * tokens
    before = [] if before is None else [before]

    def kernel(place, *refs):
        mine, deep = refs[:n], refs[n : 2 * n]
        w_mine, w_deep = refs[2 * n : 2 * n + 2]
        held, *outs = refs[2 * n + 2 + len(before) :]

        def stacked(blocks):
            return jnp.concatenate([b[...].reshape(rows, width) for b in blocks], 0)

        lhs, lhs_deep = stacked(mine), stacked(deep)
        at = [lax.rem(place[1] + d % NZ + 2 * NZ - 2 * place[3], NZ) for d in distances]
        for g in range(4):
            cols = slice(g * tile, (g + 1) * tile)
            part = jnp.dot(lhs, w_mine[:, cols], preferred_element_type=F32)
            part += jnp.dot(lhs_deep, w_deep[:, cols], preferred_element_type=F32)
            for i in range(n):
                held[at[i], :, cols] = part[i * rows : (i + 1) * rows]
        for k, out in enumerate(outs):
            s, cols = (0, slice(0, half)) if k == 0 else ((k + 1) // 2, slice((k - 1) % 2 * half // 2, ((k - 1) % 2 + 1) * half // 2))
            for p in range(2):
                out[p * rows : (p + 1) * rows, :] = held[2 * s + p, :, cols]

    shapes = [jax.ShapeDtypeStruct((NZ, rows, half), F32)]
    if last:
        shapes += [jax.ShapeDtypeStruct((2 * rows, half), F32)]
        shapes += [jax.ShapeDtypeStruct((2 * rows, half // 2), F32)] * (2 * NX - 2)
    out = call(
        kernel,
        shapes,
        place,
        *mine,
        *deep,
        w_mine,
        w_deep,
        *before,
        aliases={3 + 2 * n: 0} if before else None,
    )
    return out[1:] if last else out[0]


def half_of(place, value, mine):
    half = value.shape[-1] // 2

    def kernel(place, value, out):
        core = place[0] if mine else 1 - place[0]
        out[...] = value[..., pl.ds(pl.multiple_of(core * half, half), half)]

    return call(kernel, jax.ShapeDtypeStruct((*value.shape[:-1], half), value.dtype), place, value)


def halves_of(place, value):
    rows, half = value.shape[0], value.shape[1] // 2

    def kernel(place, value, mine, theirs, sem):
        copies = [
            pltpu.make_async_copy(
                value.at[:, pl.ds(pl.multiple_of(core * half, half), half)], out, sem.at[k]
            )
            for k, (core, out) in enumerate(((1 - place[0], theirs), (place[0], mine)))
        ]
        for copy in copies:
            copy.start()
        for copy in copies:
            copy.wait()

    in_vmem = pl.BlockSpec(memory_space=pltpu.VMEM)
    return pl.pallas_call(
        kernel,
        out_shape=[jax.ShapeDtypeStruct((rows, half), value.dtype)] * 2,
        in_specs=[pl.BlockSpec(memory_space=pltpu.SMEM), pl.BlockSpec(memory_space=pl.ANY)],
        out_specs=[in_vmem] * 2,
        scratch_shapes=[pltpu.SemaphoreType.DMA((2,))],
        cost_estimate=pl.CostEstimate(flops=0, bytes_accessed=0, transcendentals=0),
    )(place, value)


def teacher_rows(place, at, mine, theirs):
    rows = mine.shape[0]
    inside = slice(at.start % rows, at.start % rows + at.stop - at.start)
    return jnp.where(place[0] == at.start // rows, mine[inside, :], theirs[inside, :]).astype(F32)


def row_statistics(place, own, terms, teachers):
    rows, half = own.shape
    step = 32

    def kernel(place, own, a, b, c, d, teacher, theirs, student, out, held):
        lane = lax.broadcasted_iota(jnp.int32, (step, 128), 1)
        for i in range(rows // step):
            at = slice(i * step, (i + 1) * step)
            s = own[at, :] + jnp.concatenate([a[at, :] + b[at, :], c[at, :] + d[at, :]], 1)
            t = teacher_rows(place, at, teacher, theirs)
            top_s = jnp.max(s, axis=1, keepdims=True)
            top_t = jnp.max(t, axis=1, keepdims=True)
            e = jnp.exp(s - top_s)
            values = (
                top_s,
                jnp.sum(e, axis=1, keepdims=True),
                jnp.sum(e * (s - t), axis=1, keepdims=True),
                top_t,
                jnp.sum(jnp.exp(t - top_t), axis=1, keepdims=True),
            )
            stats = jnp.zeros((step, 128), F32)
            for k, v in enumerate(values):
                stats = jnp.where(lane == k, v, stats)
            student[at, :] = s
            held[at, :] = stats
        out[...] = held[...].T[:8]

    return call(
        kernel,
        [jax.ShapeDtypeStruct((rows, half), F32), jax.ShapeDtypeStruct((8, rows), F32)],
        place,
        own,
        *terms,
        *teachers,
        scratch=[pltpu.VMEM((rows, 128), F32)],
    )


def merged(parts):
    top_s = jnp.max(parts[0], axis=0, keepdims=True)
    top_t = jnp.max(parts[3], axis=0, keepdims=True)
    scale_s, scale_t = jnp.exp(parts[0] - top_s), jnp.exp(parts[3] - top_t)
    return (
        top_s,
        jnp.sum(parts[1] * scale_s, axis=0, keepdims=True),
        jnp.sum(parts[2] * scale_s, axis=0, keepdims=True),
        top_t,
        jnp.sum(parts[4] * scale_t, axis=0, keepdims=True),
    )


def merge_cores(place, mine, theirs, copies):
    def kernel(place, mine, theirs, out):
        first = place[0] == 0
        a = jnp.where(first, mine[...], theirs[...])
        b = jnp.where(first, theirs[...], mine[...])
        rows = merged([jnp.concatenate([a[k : k + 1], b[k : k + 1]], 0) for k in range(5)])
        row = lax.broadcasted_iota(jnp.int32, a.shape, 0)
        value = jnp.zeros(a.shape, F32)
        for k, v in enumerate(rows):
            value = jnp.where(row == k, v, value)
        for k in range(copies):
            out[k] = value

    return call(kernel, jax.ShapeDtypeStruct((copies, *mine.shape), F32), place, mine, theirs)


def gradients(place, shares, student, teachers):
    rows, half = student.shape
    step = 32

    def kernel(place, shares, student, teacher, theirs, out, kl_sum, held):
        top_s, total_s, spread, top_t, total_t = merged([shares[:, k, :] for k in range(5)])
        lse_s, lse_t = top_s + jnp.log(total_s), top_t + jnp.log(total_t)
        kl = spread / total_s - lse_s + lse_t
        kl_sum[...] = jnp.broadcast_to(jnp.sum(kl, axis=1, keepdims=True), kl_sum.shape)
        row = lax.broadcasted_iota(jnp.int32, (128, rows), 0)
        held[...] = jnp.where(row == 0, lse_s, jnp.where(row == 1, lse_t - lse_s - kl, 0.0)).T
        for i in range(rows // step):
            at = slice(i * step, (i + 1) * step)
            lse, add = held[at, 0:1], held[at, 1:2]
            s = student[at, :]
            t = teacher_rows(place, at, teacher, theirs)
            out[at, :] = (16.0 * jnp.exp(s - lse) * (s - t + add)).astype(out.dtype)

    return call(
        kernel,
        [jax.ShapeDtypeStruct((rows, half), BF16), jax.ShapeDtypeStruct((8, 128), F32)],
        place,
        shares,
        student,
        *teachers,
        scratch=[pltpu.VMEM((rows, 128), F32)],
    )


def panel_transposed(place, distances, blocks):
    owners, tokens, width = blocks[0].shape
    rows = owners * tokens

    def kernel(place, *refs):
        held, out = refs[:-1], refs[-1]
        for d, block in zip(distances, held):
            at = lax.rem(place[1] + d % NZ + 2 * NZ - 2 * place[3], NZ)
            out[:, pl.ds(pl.multiple_of(at * rows, rows), rows)] = block[...].reshape(rows, width).T

    shape = jax.ShapeDtypeStruct((width, len(blocks) * rows), BF16)
    return call(kernel, shape, place, *blocks)


def hidden_parts(place, steps, mine, deep, w_mine, w_theirs, before, tile=256):
    n, (rows, half) = len(steps), mine[0].shape
    width = w_mine.shape[0]
    tile = min(tile, width // 2)
    tokens = rows // (2 * NY)
    kept = ((0, 0), (0, 1), (1, 0), (3, 1))
    before = before or []

    def kernel(place, *refs):
        mine, deep = refs[:n], refs[n : 2 * n]
        w_mine, w_theirs = refs[2 * n : 2 * n + 2]
        *outs, lhs, lhs_deep = refs[2 * n + 2 + len(before) :]
        pieces = [(i, k) for i in range(n) for k in range(2)]
        for s in range(NY):
            y = lax.rem(place[2] + s, NY)
            for m, (i, k) in enumerate(pieces):
                at = pl.ds(pl.multiple_of((k * NY + y) * tokens, tokens), tokens)
                to = (s * len(pieces) + m) * tokens
                lhs[to : to + tokens, :] = mine[i][at, :]
                lhs_deep[to : to + tokens, :] = deep[i][at, :]
        away = [lax.rem(2 * place[3] + 2 * steps[i] + k + NZ - place[1], NZ) for i, k in pieces]
        contract = (((1,), (1,)), ((), ()))
        for g in range(width // tile):
            at = slice(g * tile, (g + 1) * tile)
            out = lax.dot_general(lhs[...], w_mine[at, :], contract, preferred_element_type=F32)
            out += lax.dot_general(lhs_deep[...], w_theirs[at, :], contract, preferred_element_type=F32)
            h, col = divmod(g * tile, width // 2)
            for s in range(NY):
                ref = outs[2 * s + h]
                for m, d in enumerate(away):
                    to = pl.ds(pl.multiple_of(d * tokens, tokens), tokens)
                    row = (s * len(pieces) + m) * tokens
                    ref[to, col : col + tile] = out[row : row + tokens].astype(ref.dtype)

    return call(
        kernel,
        [
            jax.ShapeDtypeStruct((rows, width // 2), F32 if (s, k) in kept else BF16)
            for s in range(NY)
            for k in range(2)
        ],
        place,
        *mine,
        *deep,
        w_mine,
        w_theirs,
        *before,
        scratch=[pltpu.VMEM((n * rows, half), BF16)] * 2,
        aliases={3 + 2 * n + k: k for k in range(len(before))},
    )


def head_product(place, panel, grads, other, before=None, tile=256):
    width, total = panel.shape
    n, (rows, half) = len(grads), grads[0].shape
    tile = min(tile, width)
    before = [] if before is None else [before]

    def kernel(place, panel, *refs):
        grads, out, held = refs[:n], refs[n + len(before)], refs[-1]

        @pl.when(pl.program_id(0) == 0)
        def _():
            for k in range(n):
                held[k * rows : (k + 1) * rows, :] = grads[k][...]

        out[...] = jnp.dot(panel[...], held[...], preferred_element_type=F32).astype(out.dtype)

    in_vmem = pl.BlockSpec(memory_space=pltpu.VMEM)
    return pl.pallas_call(
        kernel,
        out_shape=jax.ShapeDtypeStruct((width, 2 * half), BF16),
        grid_spec=pltpu.PrefetchScalarGridSpec(
            num_scalar_prefetch=1,
            grid=(width // tile,),
            in_specs=[pl.BlockSpec((tile, total), lambda i, place: (i, 0))]
            + [in_vmem] * n
            + [pl.BlockSpec(memory_space=pl.ANY)] * len(before),
            out_specs=pl.BlockSpec(
                (tile, half), lambda i, place: (i, other + place[0] - 2 * other * place[0])
            ),
            scratch_shapes=[pltpu.VMEM((total, half), BF16)],
        ),
        input_output_aliases={2 + n: 0} if before else {},
        compiler_params=pltpu.CompilerParams(vmem_limit_bytes=24 * MIB),
        cost_estimate=pl.CostEstimate(flops=0, bytes_accessed=0, transcendentals=0),
    )(place, panel, *grads, *before)


def per_device(h, w, t):
    x, c, z, y = (lax.axis_index(a) for a in ("x", "c", "z", "y"))
    tokens, width = h.shape
    half = w.shape[1] // 2
    place = jnp.stack([c, z, y, x]).astype(jnp.int32)

    near = [h] + [from_offset(h, "y", s, NY) for s in (1, 2, 3)]
    w_mine, w_theirs = halves_of(place, w)
    near, w_mine, w_theirs = held(near, w_mine, w_theirs)
    near = by_y(place, near)
    w_deep = swap(w_theirs)

    def products(distances, new, parts, last=False):
        blocks.update(zip(distances, new))
        deep = [swap(b) for b in new]
        return student_parts(place, distances, new, deep, w_mine, w_deep, parts, last)

    blocks, parts = {}, None
    up, down = from_offset(near, "z", -1, NZ), from_offset(near, "z", 1, NZ)
    distances, new = (0, -1, 1), [near, up, down]
    for step in (2, 3):
        up, down = from_offset(up, "z", -1, NZ), from_offset(down, "z", 1, NZ)
        parts = products(distances, new, parts)
        up, down, parts, t = held(up, down, parts, t)
        distances, new = (-step, step), [up, down]
    far = [from_offset(up[:2], "z", -1, NZ), from_offset(down[2:], "z", 1, NZ)]
    teachers = half_of(place, t, True), swap(half_of(place, t, False))
    far, teachers = held(far, teachers)
    parts = products((*distances, 4), new + [jnp.concatenate(far, 0)], parts, True)

    own, right_a, right_b, two_a, two_b, left_a, left_b = parts
    two_a, two_b = from_offset(two_a, "x", -1, NX), from_offset(two_b, "x", 1, NX)
    two_a, two_b, panel = ordered(two_a, two_b, panel_transposed(place, list(blocks), list(blocks.values())))
    terms = (
        from_offset(right_a + two_a, "x", -1, NX),
        from_offset(left_a, "x", 1, NX),
        from_offset(right_b, "x", -1, NX),
        from_offset(left_b + two_b, "x", 1, NX),
    )
    student, mine = row_statistics(place, own, terms, teachers)

    copies = merge_cores(place, mine, swap(mine), NZ * NY)
    shares = lax.all_to_all(copies, ("z", "y"), 0, 0, tiled=True)
    grad, kl_sum = gradients(place, shares, student, teachers)

    mine = [grad] + [from_offset(grad, "x", s, NX) for s in (1, 2, 3)]
    deep = [swap(g) for g in mine]
    sums = None
    for steps in ((0, 1, 3), (2,)):
        near_x = [mine[j] for j in steps], [deep[j] for j in steps]
        sums = hidden_parts(place, steps, *near_x, w_mine, w_theirs, sums)
    own, one, two, three = list(sums[:2]), sums[2:4], sums[4:6], sums[6:]
    two = [from_offset(two[0], "y", -1, NY), from_offset(two[1], "y", 1, NY)]
    kl_sum, own[0] = ordered(kl_sum, own[0])
    kl_sum = kl_sum + lax.ppermute(kl_sum, "x", [(i ^ 1, i) for i in range(NX)])
    two, kl_sum = held(two, kl_sum)
    kl_sum = kl_sum + lax.ppermute(kl_sum, "x", [(i ^ 2, i) for i in range(NX)])
    head_grad = head_product(place, panel, mine, 0)
    came = [[None, from_offset(one[1], "y", -1, NY)], [from_offset(three[0], "y", 1, NY), None]]
    one = (one[0] + two[0].astype(F32)).astype(BF16)
    three = (three[1] + two[1].astype(F32)).astype(BF16)
    came[0][0], came[1][1] = from_offset(one, "y", -1, NY), from_offset(three, "y", 1, NY)
    head_grad = head_product(place, panel, deep, 1, head_grad)
    came, head_grad, kl_sum = held(came, head_grad, kl_sum)
    loss = kl_sum[0, 0] / (NX * NZ * tokens)
    total = jnp.concatenate(
        [own[k] + came[0][k].astype(F32) + came[1][k].astype(F32) for k in range(2)], 1
    )
    hidden_grad = None
    for d in (0, 4, 3, 5, 2, 6, 1, 7):
        piece = total[d * tokens : (d + 1) * tokens]
        if d:
            piece = from_offset(piece.astype(BF16), "z", -d, NZ).astype(F32)
        hidden_grad = piece if hidden_grad is None else hidden_grad + piece
    return loss, head_grad, hidden_grad.astype(BF16)


def solution(mesh):
    fine = Mesh(mesh.devices.reshape(NX, NC, NZ, NY), ("x", "c", "z", "y"))
    row, col = ("x", "c"), ("z", "y")
    return jax.shard_map(
        per_device,
        mesh=fine,
        in_specs=(P(col, row), P(row, col), P(row, col)),
        out_specs=(P(), P(row, col), P(col, row)),
        check_vma=False,
    )
```

```python
import jax
import jax.numpy as jnp
from jax import lax
from jax.experimental import pallas as pl
from jax.experimental.pallas import tpu as pltpu
from jax.sharding import Mesh, PartitionSpec as P

NX, NC, NZ, NY = 4, 2, 8, 4
F32, BF16 = jnp.float32, jnp.bfloat16
MIB = 2**20


def from_offset(value, axis, offset, size):
    return lax.ppermute(value, axis, [((i + offset) % size, i) for i in range(size)])


def swap(value):
    return lax.ppermute(value, "c", [(0, 1), (1, 0)])


def ordered(*values):
    return lax.optimization_barrier(values)


def held(*trees):
    leaves, shape = jax.tree.flatten(trees)
    return jax.tree.unflatten(shape, ordered(*leaves))


def call(kernel, out_shape, place, *args, scratch=(), aliases=None, vmem=10 * MIB):
    in_vmem = pl.BlockSpec(memory_space=pltpu.VMEM)
    return pl.pallas_call(
        kernel,
        out_shape=out_shape,
        in_specs=[pl.BlockSpec(memory_space=pltpu.SMEM)] + [in_vmem] * len(args),
        out_specs=jax.tree.map(lambda _: in_vmem, out_shape),
        scratch_shapes=list(scratch),
        input_output_aliases=aliases or {},
        compiler_params=pltpu.CompilerParams(vmem_limit_bytes=vmem),
        cost_estimate=pl.CostEstimate(flops=0, bytes_accessed=0, transcendentals=0),
    )(place, *args)


def by_y(place, values):
    def kernel(place, *refs):
        for s, value in enumerate(refs[:-1]):
            refs[-1][lax.rem(s + place[2], NY)] = value[...]

    shape = (len(values), *values[0].shape)
    return call(kernel, jax.ShapeDtypeStruct(shape, values[0].dtype), place, *values)


def student_parts(place, distances, mine, deep, w_mine, w_deep, before, last):
    n, (_, tokens, width) = len(mine), mine[0].shape
    half = w_deep.shape[1]
    tile = half // 4
    rows = NY * tokens
    before = [] if before is None else [before]

    def kernel(place, *refs):
        mine, deep = refs[:n], refs[n : 2 * n]
        w_mine, w_deep = refs[2 * n : 2 * n + 2]
        held, *outs = refs[2 * n + 2 + len(before) :]

        def stacked(blocks):
            return jnp.concatenate([b[...].reshape(rows, width) for b in blocks], 0)

        lhs, lhs_deep = stacked(mine), stacked(deep)
        at = [lax.rem(place[1] + d % NZ + 2 * NZ - 2 * place[3], NZ) for d in distances]
        for g in range(4):
            cols = slice(g * tile, (g + 1) * tile)
            part = jnp.dot(lhs, w_mine[:, cols], preferred_element_type=F32)
            part += jnp.dot(lhs_deep, w_deep[:, cols], preferred_element_type=F32)
            for i in range(n):
                held[at[i], :, cols] = part[i * rows : (i + 1) * rows]
        for k, out in enumerate(outs):
            s, cols = (0, slice(0, half)) if k == 0 else ((k + 1) // 2, slice((k - 1) % 2 * half // 2, ((k - 1) % 2 + 1) * half // 2))
            for p in range(2):
                out[p * rows : (p + 1) * rows, :] = held[2 * s + p, :, cols]

    shapes = [jax.ShapeDtypeStruct((NZ, rows, half), F32)]
    if last:
        shapes += [jax.ShapeDtypeStruct((2 * rows, half), F32)]
        shapes += [jax.ShapeDtypeStruct((2 * rows, half // 2), F32)] * (2 * NX - 2)
    out = call(
        kernel,
        shapes,
        place,
        *mine,
        *deep,
        w_mine,
        w_deep,
        *before,
        aliases={3 + 2 * n: 0} if before else None,
    )
    return out[1:] if last else out[0]


def half_of(place, value, mine):
    half = value.shape[-1] // 2

    def kernel(place, value, out):
        core = place[0] if mine else 1 - place[0]
        out[...] = value[..., pl.ds(pl.multiple_of(core * half, half), half)]

    return call(kernel, jax.ShapeDtypeStruct((*value.shape[:-1], half), value.dtype), place, value)


def halves_of(place, value):
    rows, half = value.shape[0], value.shape[1] // 2

    def kernel(place, value, mine, theirs, sem):
        copies = [
            pltpu.make_async_copy(
                value.at[:, pl.ds(pl.multiple_of(core * half, half), half)], out, sem.at[k]
            )
            for k, (core, out) in enumerate(((1 - place[0], theirs), (place[0], mine)))
        ]
        for copy in copies:
            copy.start()
        for copy in copies:
            copy.wait()

    in_vmem = pl.BlockSpec(memory_space=pltpu.VMEM)
    return pl.pallas_call(
        kernel,
        out_shape=[jax.ShapeDtypeStruct((rows, half), value.dtype)] * 2,
        in_specs=[pl.BlockSpec(memory_space=pltpu.SMEM), pl.BlockSpec(memory_space=pl.ANY)],
        out_specs=[in_vmem] * 2,
        scratch_shapes=[pltpu.SemaphoreType.DMA((2,))],
        cost_estimate=pl.CostEstimate(flops=0, bytes_accessed=0, transcendentals=0),
    )(place, value)


def teacher_rows(place, at, mine, theirs):
    rows = mine.shape[0]
    inside = slice(at.start % rows, at.start % rows + at.stop - at.start)
    return jnp.where(place[0] == at.start // rows, mine[inside, :], theirs[inside, :]).astype(F32)


def row_statistics(place, own, terms, teachers):
    rows, half = own.shape
    step = 32

    def kernel(place, own, a, b, c, d, teacher, theirs, student, out, held):
        lane = lax.broadcasted_iota(jnp.int32, (step, 128), 1)
        for i in range(rows // step):
            at = slice(i * step, (i + 1) * step)
            s = own[at, :] + jnp.concatenate([a[at, :] + b[at, :], c[at, :] + d[at, :]], 1)
            t = teacher_rows(place, at, teacher, theirs)
            top_s = jnp.max(s, axis=1, keepdims=True)
            top_t = jnp.max(t, axis=1, keepdims=True)
            e = jnp.exp(s - top_s)
            values = (
                top_s,
                jnp.sum(e, axis=1, keepdims=True),
                jnp.sum(e * (s - t), axis=1, keepdims=True),
                top_t,
                jnp.sum(jnp.exp(t - top_t), axis=1, keepdims=True),
            )
            stats = jnp.zeros((step, 128), F32)
            for k, v in enumerate(values):
                stats = jnp.where(lane == k, v, stats)
            student[at, :] = s
            held[at, :] = stats
        out[...] = held[...].T[:8]

    return call(
        kernel,
        [jax.ShapeDtypeStruct((rows, half), F32), jax.ShapeDtypeStruct((8, rows), F32)],
        place,
        own,
        *terms,
        *teachers,
        scratch=[pltpu.VMEM((rows, 128), F32)],
    )


def merged(parts):
    top_s = jnp.max(parts[0], axis=0, keepdims=True)
    top_t = jnp.max(parts[3], axis=0, keepdims=True)
    scale_s, scale_t = jnp.exp(parts[0] - top_s), jnp.exp(parts[3] - top_t)
    return (
        top_s,
        jnp.sum(parts[1] * scale_s, axis=0, keepdims=True),
        jnp.sum(parts[2] * scale_s, axis=0, keepdims=True),
        top_t,
        jnp.sum(parts[4] * scale_t, axis=0, keepdims=True),
    )


def merge_cores(place, mine, theirs, copies):
    def kernel(place, mine, theirs, out):
        first = place[0] == 0
        a = jnp.where(first, mine[...], theirs[...])
        b = jnp.where(first, theirs[...], mine[...])
        rows = merged([jnp.concatenate([a[k : k + 1], b[k : k + 1]], 0) for k in range(5)])
        row = lax.broadcasted_iota(jnp.int32, a.shape, 0)
        value = jnp.zeros(a.shape, F32)
        for k, v in enumerate(rows):
            value = jnp.where(row == k, v, value)
        for k in range(copies):
            out[k] = value

    return call(kernel, jax.ShapeDtypeStruct((copies, *mine.shape), F32), place, mine, theirs)


def gradients(place, shares, student, teachers):
    rows, half = student.shape
    step = 32

    def kernel(place, shares, student, teacher, theirs, out, kl_sum, held):
        top_s, total_s, spread, top_t, total_t = merged([shares[:, k, :] for k in range(5)])
        lse_s, lse_t = top_s + jnp.log(total_s), top_t + jnp.log(total_t)
        kl = spread / total_s - lse_s + lse_t
        kl_sum[...] = jnp.broadcast_to(jnp.sum(kl, axis=1, keepdims=True), kl_sum.shape)
        row = lax.broadcasted_iota(jnp.int32, (128, rows), 0)
        held[...] = jnp.where(row == 0, lse_s, jnp.where(row == 1, lse_t - lse_s - kl, 0.0)).T
        for i in range(rows // step):
            at = slice(i * step, (i + 1) * step)
            lse, add = held[at, 0:1], held[at, 1:2]
            s = student[at, :]
            t = teacher_rows(place, at, teacher, theirs)
            out[at, :] = (16.0 * jnp.exp(s - lse) * (s - t + add)).astype(out.dtype)

    return call(
        kernel,
        [jax.ShapeDtypeStruct((rows, half), BF16), jax.ShapeDtypeStruct((8, 128), F32)],
        place,
        shares,
        student,
        *teachers,
        scratch=[pltpu.VMEM((rows, 128), F32)],
    )


def panel_transposed(place, distances, blocks):
    owners, tokens, width = blocks[0].shape
    rows = owners * tokens

    def kernel(place, *refs):
        held, out = refs[:-1], refs[-1]
        for d, block in zip(distances, held):
            at = lax.rem(place[1] + d % NZ + 2 * NZ - 2 * place[3], NZ)
            out[:, pl.ds(pl.multiple_of(at * rows, rows), rows)] = block[...].reshape(rows, width).T

    shape = jax.ShapeDtypeStruct((width, len(blocks) * rows), BF16)
    return call(kernel, shape, place, *blocks)


def hidden_parts(place, steps, mine, deep, w_mine, w_theirs, before, tile=256):
    n, (rows, half) = len(steps), mine[0].shape
    width = w_mine.shape[0]
    tile = min(tile, width // 2)
    tokens = rows // (2 * NY)
    kept = ((0, 0), (0, 1), (1, 0), (3, 1))
    before = before or []

    def kernel(place, *refs):
        mine, deep = refs[:n], refs[n : 2 * n]
        w_mine, w_theirs = refs[2 * n : 2 * n + 2]
        *outs, lhs, lhs_deep = refs[2 * n + 2 + len(before) :]
        pieces = [(i, k) for i in range(n) for k in range(2)]
        for s in range(NY):
            y = lax.rem(place[2] + s, NY)
            for m, (i, k) in enumerate(pieces):
                at = pl.ds(pl.multiple_of((k * NY + y) * tokens, tokens), tokens)
                to = (s * len(pieces) + m) * tokens
                lhs[to : to + tokens, :] = mine[i][at, :]
                lhs_deep[to : to + tokens, :] = deep[i][at, :]
        away = [lax.rem(2 * place[3] + 2 * steps[i] + k + NZ - place[1], NZ) for i, k in pieces]
        contract = (((1,), (1,)), ((), ()))
        for g in range(width // tile):
            at = slice(g * tile, (g + 1) * tile)
            out = lax.dot_general(lhs[...], w_mine[at, :], contract, preferred_element_type=F32)
            out += lax.dot_general(lhs_deep[...], w_theirs[at, :], contract, preferred_element_type=F32)
            h, col = divmod(g * tile, width // 2)
            for s in range(NY):
                ref = outs[2 * s + h]
                for m, d in enumerate(away):
                    to = pl.ds(pl.multiple_of(d * tokens, tokens), tokens)
                    row = (s * len(pieces) + m) * tokens
                    ref[to, col : col + tile] = out[row : row + tokens].astype(ref.dtype)

    return call(
        kernel,
        [
            jax.ShapeDtypeStruct((rows, width // 2), F32 if (s, k) in kept else BF16)
            for s in range(NY)
            for k in range(2)
        ],
        place,
        *mine,
        *deep,
        w_mine,
        w_theirs,
        *before,
        scratch=[pltpu.VMEM((n * rows, half), BF16)] * 2,
        aliases={3 + 2 * n + k: k for k in range(len(before))},
    )


def head_product(place, panel, grads, other, before=None, tile=256):
    width, total = panel.shape
    n, (rows, half) = len(grads), grads[0].shape
    tile = min(tile, width)
    before = [] if before is None else [before]

    def kernel(place, panel, *refs):
        grads, out, held = refs[:n], refs[n + len(before)], refs[-1]

        @pl.when(pl.program_id(0) == 0)
        def _():
            for k in range(n):
                held[k * rows : (k + 1) * rows, :] = grads[k][...]

        out[...] = jnp.dot(panel[...], held[...], preferred_element_type=F32).astype(out.dtype)

    in_vmem = pl.BlockSpec(memory_space=pltpu.VMEM)
    return pl.pallas_call(
        kernel,
        out_shape=jax.ShapeDtypeStruct((width, 2 * half), BF16),
        grid_spec=pltpu.PrefetchScalarGridSpec(
            num_scalar_prefetch=1,
            grid=(width // tile,),
            in_specs=[pl.BlockSpec((tile, total), lambda i, place: (i, 0))]
            + [in_vmem] * n
            + [pl.BlockSpec(memory_space=pl.ANY)] * len(before),
            out_specs=pl.BlockSpec(
                (tile, half), lambda i, place: (i, other + place[0] - 2 * other * place[0])
            ),
            scratch_shapes=[pltpu.VMEM((total, half), BF16)],
        ),
        input_output_aliases={2 + n: 0} if before else {},
        compiler_params=pltpu.CompilerParams(vmem_limit_bytes=24 * MIB),
        cost_estimate=pl.CostEstimate(flops=0, bytes_accessed=0, transcendentals=0),
    )(place, panel, *grads, *before)


def per_device(h, w, t):
    x, c, z, y = (lax.axis_index(a) for a in ("x", "c", "z", "y"))
    tokens, width = h.shape
    half = w.shape[1] // 2
    place = jnp.stack([c, z, y, x]).astype(jnp.int32)

    near = [h] + [from_offset(h, "y", s, NY) for s in (1, 2, 3)]
    w_mine, w_theirs = halves_of(place, w)
    near, w_mine, w_theirs = held(near, w_mine, w_theirs)
    near = by_y(place, near)
    w_deep = swap(w_theirs)

    def products(distances, new, parts, last=False):
        blocks.update(zip(distances, new))
        deep = [swap(b) for b in new]
        return student_parts(place, distances, new, deep, w_mine, w_deep, parts, last)

    blocks, parts = {}, None
    up, down = from_offset(near, "z", -1, NZ), from_offset(near, "z", 1, NZ)
    distances, new = (0, -1, 1), [near, up, down]
    for step in (2, 3):
        up, down = from_offset(up, "z", -1, NZ), from_offset(down, "z", 1, NZ)
        parts = products(distances, new, parts)
        up, down, parts, t = held(up, down, parts, t)
        distances, new = (-step, step), [up, down]
    far = [from_offset(up[:2], "z", -1, NZ), from_offset(down[2:], "z", 1, NZ)]
    teachers = half_of(place, t, True), swap(half_of(place, t, False))
    far, teachers = held(far, teachers)
    parts = products((*distances, 4), new + [jnp.concatenate(far, 0)], parts, True)

    own, right_a, right_b, two_a, two_b, left_a, left_b = parts
    two_a, two_b = from_offset(two_a, "x", -1, NX), from_offset(two_b, "x", 1, NX)
    two_a, two_b, panel = ordered(two_a, two_b, panel_transposed(place, list(blocks), list(blocks.values())))
    terms = (
        from_offset(right_a + two_a, "x", -1, NX),
        from_offset(left_a, "x", 1, NX),
        from_offset(right_b, "x", -1, NX),
        from_offset(left_b + two_b, "x", 1, NX),
    )
    student, mine = row_statistics(place, own, terms, teachers)

    copies = merge_cores(place, mine, swap(mine), NZ * NY)
    shares = lax.all_to_all(copies, ("z", "y"), 0, 0, tiled=True)
    grad, kl_sum = gradients(place, shares, student, teachers)

    after, before = from_offset(grad, "x", 1, NX), from_offset(grad, "x", -1, NX)
    opposite = [
        from_offset(after[:, : half // 2], "x", 1, NX),
        from_offset(before[:, half // 2 :], "x", -1, NX),
    ]
    mine = [grad, after, jnp.concatenate(opposite, 1), before]
    deep = [swap(g) for g in mine]
    sums = None
    for steps in ((0, 1, 3), (2,)):
        near_x = [mine[j] for j in steps], [deep[j] for j in steps]
        sums = hidden_parts(place, steps, *near_x, w_mine, w_theirs, sums)
    own, one, two, three = list(sums[:2]), sums[2:4], sums[4:6], sums[6:]
    two = [from_offset(two[0], "y", -1, NY), from_offset(two[1], "y", 1, NY)]
    kl_sum, own[0] = ordered(kl_sum, own[0])
    kl_sum = kl_sum + lax.ppermute(kl_sum, "x", [(i ^ 1, i) for i in range(NX)])
    two, kl_sum = held(two, kl_sum)
    kl_sum = kl_sum + lax.ppermute(kl_sum, "x", [(i ^ 2, i) for i in range(NX)])
    head_grad = head_product(place, panel, mine, 0)
    came = [[None, from_offset(one[1], "y", -1, NY)], [from_offset(three[0], "y", 1, NY), None]]
    one = (one[0] + two[0].astype(F32)).astype(BF16)
    three = (three[1] + two[1].astype(F32)).astype(BF16)
    came[0][0], came[1][1] = from_offset(one, "y", -1, NY), from_offset(three, "y", 1, NY)
    head_grad = head_product(place, panel, deep, 1, head_grad)
    came, head_grad, kl_sum = held(came, head_grad, kl_sum)
    loss = kl_sum[0, 0] / (NX * NZ * tokens)
    total = jnp.concatenate(
        [own[k] + came[0][k].astype(F32) + came[1][k].astype(F32) for k in range(2)], 1
    )
    hidden_grad = None
    for d in (0, 4, 3, 5, 2, 6, 1, 7):
        piece = total[d * tokens : (d + 1) * tokens]
        if d:
            piece = from_offset(piece.astype(BF16), "z", -d, NZ).astype(F32)
        hidden_grad = piece if hidden_grad is None else hidden_grad + piece
    return loss, head_grad, hidden_grad.astype(BF16)


def solution(mesh):
    fine = Mesh(mesh.devices.reshape(NX, NC, NZ, NY), ("x", "c", "z", "y"))
    row, col = ("x", "c"), ("z", "y")
    return jax.shard_map(
        per_device,
        mesh=fine,
        in_specs=(P(col, row), P(row, col), P(row, col)),
        out_specs=(P(), P(row, col), P(col, row)),
        check_vma=False,
    )
```
